32 devices in a mesh: row: 4 (over z), col: 8 (over y, x, core).
Axes of the slice: x: 2, y: 2, z: 4, core: 2. Of those that a mesh axis runs over, the one named last changes fastest.
Arguments:
- src_pos: float32 [3, 65536], P(None, 'row'), may hold values from 0 to 10
- tgt_pos: float32 [3, 2048], P(None, 'col'), may hold values from 0 to 20
- src_weight: float32 [65536], P('row'), may hold values from 0.1 to 3
- tgt_weight: float32 [2048], P('col'), may hold values from 0.1 to 3
- src_order: int32 [65536], P('row'), may hold values from 0 to 65535, as said below
- tgt_order: int32 [2048], P('col'), may hold values from 0 to 2047, as said below
- tile_mask: int32 [256, 8], P('row', 'col'), may hold values from 0 to 1, as said below
Outputs:
- src_potential: float32 [65536], P('row')
- tgt_potential: float32 [2048], P('col')
- displacement: float32 [3, 65536], P(None, 'row')
The draws below stay inside these ranges and needn't reach their ends.
Inputs may be any that keep to these rules, and one draw needn't show every extreme that they name: `src_order`: each aligned block of 16384 entries is a permutation of that block's own indices. `tgt_order`: each aligned block of 256 entries is a permutation of that block's own indices. `tile_mask`: every row and every column of the mask holds at least one kept pair.
All inputs are finite; a program needn't handle non-finite values.
Results may differ from the reference program's by a relative error of at most 0.0003.
Values sent between devices are 32-bit elements; how exact they have to be, the bound alone decides.
A program may use at most 64 MiB of HBM per device.

```python
import jax
import jax.numpy as jnp
from jax import lax

TILE = 256
SRC_DEV = 16384
TGT_DEV = 256
SWEEPS = 2
NSRC = 65536
NTGT = 2048


def block_shuffle(key, count, block_size):
    blocks = count // block_size
    block_keys = jax.random.split(key, blocks)

    def shuffle_one(block_key):
        return jax.random.permutation(block_key, block_size)
    shuffles = jax.vmap(shuffle_one)(block_keys)
    return (shuffles + (jnp.arange(blocks) * block_size)[:, None]).reshape(-1).astype(jnp.int32)


def tile_cells(key, tiles, per_block, salt, spread_top, narrow_low, narrow_top):
    blocks = tiles // per_block
    spread_cells = jax.random.randint(jax.random.fold_in(key, salt), (2, 3, tiles), 0, spread_top, dtype=jnp.int32)
    narrow_cells = jax.random.randint(jax.random.fold_in(key, salt + 1), (2, 3, tiles), narrow_low, narrow_top, dtype=jnp.int32)
    crowded = jax.random.randint(jax.random.fold_in(key, salt + 2), (blocks,), 0, 2, dtype=jnp.int32)
    crowded = jnp.repeat(crowded, per_block)
    return jnp.where(crowded[None, None, :] == 1, narrow_cells, spread_cells)


def source_cells(key):
    return tile_cells(key, NSRC // TILE, SRC_DEV // TILE, 20, 4, 1, 3)


def target_cells(key):
    tiles = NTGT // TILE
    per_block = TGT_DEV // TILE
    cells = tile_cells(key, tiles, per_block, 30, 5, 1, 4)
    far_block = jax.random.randint(jax.random.fold_in(key, 33), (), 0, NTGT // TGT_DEV, dtype=jnp.int32)
    far_tiles = jnp.arange(tiles, dtype=jnp.int32) // per_block == far_block
    return jnp.where(far_tiles[None, None, :], 7, cells)


def clustered(key, cells, order, salt):
    inverse = jnp.argsort(order, stable=True).astype(jnp.int32)
    count = order.shape[0]
    tile_of = inverse // TILE
    branch = jax.random.randint(jax.random.fold_in(key, salt + 2), (count,), 0, 2, dtype=jnp.int32)
    first = jnp.take(cells[0], tile_of, axis=1)
    second = jnp.take(cells[1], tile_of, axis=1)
    own_cells = jnp.where(branch[None, :] == 0, first, second).astype(jnp.float32)
    centre = 1.25 + 2.5 * own_cells
    jitter = jax.random.uniform(jax.random.fold_in(key, salt), (3, count), jnp.float32, -1.25, 1.25)
    return centre + jitter


def draw_src_order(key, part):
    return block_shuffle(jax.random.fold_in(key, 9), NSRC, SRC_DEV)


def draw_tgt_order(key, part):
    return block_shuffle(jax.random.fold_in(key, 10), NTGT, TGT_DEV)


def draw_src_pos(key, part):
    return clustered(key, source_cells(key), draw_src_order(key, part), 41)


def draw_tgt_pos(key, part):
    return clustered(key, target_cells(key), draw_tgt_order(key, part), 51)


def rising_mass(key, count):
    rising = 1.0 + 2.0 * jnp.arange(count, dtype=jnp.float32) / (count - 1)
    factor = jnp.exp(jax.random.uniform(key, (count,), jnp.float32, jnp.log(0.2), 0.0))
    return factor * rising


def draw_src_weight(key, part):
    return rising_mass(jax.random.fold_in(key, 7), NSRC)


def draw_tgt_weight(key, part):
    return rising_mass(jax.random.fold_in(key, 8), NTGT)


def draw_tile_mask(key, part):
    src_tiles = NSRC // TILE
    tgt_tiles = NTGT // TILE
    src_cells = source_cells(key)
    tgt_cells = target_cells(key)
    differ = jnp.abs(src_cells[:, None, :, :, None] - tgt_cells[None, :, :, None, :])
    apart = jnp.min(jnp.max(differ, axis=2), axis=(0, 1))
    kept_pairs = apart <= 1
    row_partner = jax.random.permutation(jax.random.fold_in(key, 14), src_tiles) % tgt_tiles
    col_partner = jax.random.permutation(jax.random.fold_in(key, 15), tgt_tiles) % src_tiles
    forced = (jnp.arange(tgt_tiles)[None, :] == row_partner[:, None]) | (jnp.arange(src_tiles)[:, None] == col_partner[None, :])
    return (kept_pairs | forced).astype(jnp.int32)


def setup_inputs(seed: int = 0) -> dict:
    key_of = jax.random.split(jax.random.key(seed), 8)
    src_pos = draw_src_pos(jax.random.fold_in(key_of[7], 71), 0)
    tgt_pos = draw_tgt_pos(jax.random.fold_in(key_of[7], 71), 0)
    src_weight = draw_src_weight(jax.random.fold_in(key_of[7], 71), 0)
    tgt_weight = draw_tgt_weight(jax.random.fold_in(key_of[7], 71), 0)
    src_order = draw_src_order(jax.random.fold_in(key_of[7], 71), 0)
    tgt_order = draw_tgt_order(jax.random.fold_in(key_of[7], 71), 0)
    tile_mask = draw_tile_mask(jax.random.fold_in(key_of[7], 71), 0)
    return dict(src_pos=src_pos, tgt_pos=tgt_pos, src_weight=src_weight, tgt_weight=tgt_weight, src_order=src_order, tgt_order=tgt_order, tile_mask=tile_mask)


epsilon = 0.4
lowest = -1e30


def reference(src_pos, tgt_pos, src_weight, tgt_weight, src_order, tgt_order, tile_mask):
    sources = jnp.take(src_pos, src_order, axis=1)
    targets = jnp.take(tgt_pos, tgt_order, axis=1)
    src_mass = jnp.take(src_weight, src_order)
    tgt_mass = jnp.take(tgt_weight, tgt_order)
    log_a = jnp.log(src_mass) - jnp.log(jnp.sum(src_mass))
    log_b = jnp.log(tgt_mass) - jnp.log(jnp.sum(tgt_mass))
    tile_rows = NSRC // TILE
    src_blocks = sources.reshape(3, tile_rows, TILE).transpose(1, 0, 2)
    keep_rows = jnp.repeat(tile_mask, TILE, axis=1) > 0

    def one_pass(src_field, tgt_field, with_shift):
        toward_terms = log_b + tgt_field / epsilon
        back_rows = (log_a + src_field / epsilon).reshape(tile_rows, TILE)

        def visit(carried, slices):
            col_top, col_sum = carried
            src_block, back_row, keep_row = slices
            distance = 0.5 * sum((src_block[coordinate][:, None] - targets[coordinate][None, :]) ** 2 for coordinate in range(3))
            toward = toward_terms[None, :] - distance / epsilon
            backward = back_row[:, None] - distance / epsilon
            alive = keep_row[None, :]
            row_top = jnp.max(jnp.where(alive, toward, lowest), axis=1)
            row_exp = jnp.where(alive, jnp.exp(toward - row_top[:, None]), 0.0)
            row_sum = jnp.sum(row_exp, axis=1)
            if with_shift:
                pulled = jnp.dot(row_exp, targets.T, precision=lax.Precision.HIGHEST).T
            else:
                pulled = jnp.zeros((3, TILE), jnp.float32)
            col_peak = jnp.max(jnp.where(alive, backward, lowest), axis=0)
            renewed = jnp.maximum(col_top, col_peak)
            col_sum = col_sum * jnp.exp(col_top - renewed) + jnp.sum(jnp.where(alive, jnp.exp(backward - renewed[None, :]), 0.0), axis=0)
            return (renewed, col_sum), (row_top, row_sum, pulled)

        starting = (jnp.full((NTGT,), lowest, jnp.float32), jnp.zeros((NTGT,), jnp.float32))
        (col_top, col_sum), (row_top, row_sum, pulled) = lax.scan(visit, starting, (src_blocks, back_rows, keep_rows))
        row_top = row_top.reshape(-1)
        row_sum = row_sum.reshape(-1)
        src_new = -epsilon * (row_top + jnp.log(row_sum))
        tgt_new = -epsilon * (col_top + jnp.log(col_sum))
        shift = sources - pulled.transpose(1, 0, 2).reshape(3, -1) / row_sum[None, :]
        return src_new, tgt_new, shift

    zero_src = jnp.zeros((NSRC,), jnp.float32)
    zero_tgt = jnp.zeros((NTGT,), jnp.float32)
    src_field, tgt_field, unused = one_pass(zero_src, zero_tgt, False)
    for sweep_at in range(SWEEPS):
        src_new, tgt_new, unused = one_pass(src_field, tgt_field, False)
        src_field = 0.5 * (src_field + src_new)
        tgt_field = 0.5 * (tgt_field + tgt_new)
    src_potential, tgt_potential, displacement = one_pass(src_field, tgt_field, True)
    return src_potential, tgt_potential, displacement
```

```python
import functools
import math

import jax
import jax.numpy as jnp
from jax import lax
from jax.experimental import pallas as pl
from jax.experimental.pallas import tpu as pltpu
from jax.sharding import PartitionSpec as P

TILE = 256
SWEEPS = 2
LANES = 128
FEATURES = 32

epsilon = 0.4
lowest = -1e30
middle = 5.0
log2e = math.log2(math.e)
scale = 0.5 * log2e / epsilon
MESH = pl.DeviceIdType.MESH


def rounded(x):
    return x.astype(jnp.bfloat16).astype(jnp.float32)


def three(x):
    high = rounded(x)
    mid = rounded(x - high)
    return high, mid, rounded(x - high - mid)


def columns_of(row):
    return jnp.broadcast_to(row, (LANES, row.shape[1])).T


def kernel(
    rows, cols,
    src_pos, src_weight, src_order, tgt_pos, tgt_weight, tgt_order, mask,
    src_out, tgt_out, move_out,
    table, feature, tgt_parts, tgt_feature, points, masses, cost, term, place,
    col_top, col_sum, field, own, moved,
    send_0, send_1, send_2, send_3, take_0, take_1, take_2, take_3, col_send, col_take,
    part_out, part_in, whole_out, whole_in, cross_out, cross_in,
):
    row_at = lax.axis_index("row")
    col_at = lax.axis_index("col")
    sends = (send_0, send_1, send_2, send_3)
    takes = (take_0, take_1, take_2, take_3)
    groups = src_order.shape[0]
    width = tgt_pos.shape[1]
    spans = width // LANES
    owned = field.shape[2]
    chunk = min(8, owned)
    pieces = owned // chunk
    passes = SWEEPS + 2

    barrier = pltpu.get_barrier_semaphore()
    for step in range(1, cols):
        pl.semaphore_signal(
            barrier, inc=1, device_id=(row_at, lax.rem(col_at + step, cols)), device_id_type=MESH
        )
    for step in range(1, rows):
        pl.semaphore_signal(
            barrier, inc=1, device_id=(lax.rem(row_at + step, rows), col_at), device_id_type=MESH
        )

    for entry in range(4):
        value = tgt_weight[...] if entry == 3 else tgt_pos[entry:entry + 1, :] - middle
        for at, part in enumerate(three(value)):
            tgt_parts[4 * at + entry:4 * at + entry + 1, :] = part
    tgt_parts[12:16, :] = jnp.zeros((4, width), jnp.float32)
    chosen = lax.broadcasted_iota(jnp.int32, (width, width), 0) == tgt_order[...] - col_at * width
    picked = jnp.dot(
        tgt_parts[...].astype(jnp.bfloat16),
        chosen.astype(jnp.float32).astype(jnp.bfloat16),
        preferred_element_type=jnp.float32,
    )
    picked = picked[0:4] + picked[4:8] + picked[8:12]
    tgt_feature[...] = jnp.zeros(tgt_feature.shape, jnp.float32)
    norm = jnp.zeros((1, width), jnp.float32)
    for axis in range(3):
        y = picked[axis:axis + 1]
        norm = norm - scale * y * y
        high, mid, low = three(2.0 * scale * y)
        for at, part in enumerate((high, mid, high, low, high, mid)):
            tgt_feature[6 * axis + at:6 * axis + at + 1, :] = part
        place[axis] = columns_of(y)
    for at, part in enumerate(three(norm)):
        tgt_feature[18 + at:19 + at, :] = part
    tgt_feature[21:25, :] = jnp.ones((4, width), jnp.float32)
    tgt_log = jnp.log2(picked[3:4])
    term[...] = columns_of(tgt_log)
    tgt_side = tgt_feature[...].T[:, :FEATURES].astype(jnp.bfloat16)
    tgt_local = jnp.sum(tgt_weight[...], axis=1, keepdims=True)
    src_local = jnp.sum(jnp.sum(src_weight[...], axis=1, keepdims=True), axis=0, keepdims=True)

    for entry in range(4):
        value = src_weight[...] if entry == 3 else src_pos[entry] - middle
        value = value.T
        high = rounded(value)
        span = slice(entry * LANES, (entry + 1) * LANES)
        table[span, 0:groups] = high.astype(jnp.bfloat16)
        table[span, groups:2 * groups] = (value - high).astype(jnp.bfloat16)
    feature[...] = jnp.zeros(feature.shape, jnp.float32)
    batch = feature.shape[1] // LANES

    def fetch(at, carried):
        index = jnp.concatenate(
            [src_order[pl.ds(at * batch + g, 1), :] for g in range(batch)], axis=1
        ) - row_at * (groups * LANES)
        lanes = batch * LANES
        high_at = lax.shift_right_logical(index, 7)
        low_at = lax.bitwise_and(index, LANES - 1)
        hot = lax.broadcasted_iota(jnp.int32, (groups, lanes), 0) == high_at
        hot = hot.astype(jnp.float32).astype(jnp.bfloat16)
        found = jnp.dot(
            table[...], jnp.concatenate([hot, hot], axis=0), preferred_element_type=jnp.float32
        )
        near = lax.broadcasted_iota(jnp.int32, (LANES, lanes), 0) == low_at
        values = [
            jnp.sum(
                jnp.where(near, found[entry * LANES:(entry + 1) * LANES], 0.0),
                axis=0, keepdims=True,
            )
            for entry in range(4)
        ]
        norm = jnp.zeros((1, lanes), jnp.float32)
        for axis in range(3):
            x = values[axis]
            norm = norm - scale * x * x
            high, mid, low = three(x)
            for row, part in enumerate((high, high, mid, high, low, mid)):
                feature[6 * axis + row:6 * axis + row + 1, :] = part
        feature[18:21, :] = jnp.ones((3, lanes), jnp.float32)
        for row, part in enumerate(three(norm)):
            feature[21 + row:22 + row, :] = part
        for tile in range(lanes // TILE):
            kept = mask[pl.ds(at * (lanes // TILE) + tile, 1), :]
            feature[24:25, tile * TILE:(tile + 1) * TILE] = jnp.broadcast_to(
                jnp.where(kept > 0, 0.0, lowest), (1, TILE)
            )
        near_cost = jnp.dot(
            tgt_side, feature[...].astype(jnp.bfloat16), preferred_element_type=jnp.float32
        )
        mass = jnp.log2(values[3])
        for g in range(batch):
            group = at * batch + g
            span = slice(g * LANES, (g + 1) * LANES)
            cost[group] = near_cost[:, span]
            for axis in range(3):
                points[axis, group // owned, pl.ds(lax.rem(group, owned), 1), :] = (
                    values[axis][:, span]
                )
            masses[group // owned, pl.ds(lax.rem(group, owned), 1), :] = mass[:, span]
        return carried

    lax.fori_loop(0, groups // batch, fetch, 0)
    field[0] = masses[...]

    pl.semaphore_wait(barrier, rows + cols - 2)

    src_log_total = None
    tgt_log_total = None
    tgt_field = None
    for turn in range(passes):
        closing = turn == passes - 1
        send = sends[turn]
        take = takes[turn]
        col_top[...] = jnp.full(col_top.shape, lowest, jnp.float32)
        col_sum[...] = jnp.zeros(col_sum.shape, jnp.float32)

        def visit(peer, piece, turn=turn, closing=closing, send=send):
            base = peer * owned + piece * chunk
            back = jnp.stack([
                jnp.broadcast_to(field[turn, peer, pl.ds(piece * chunk + g, 1), :], (8, LANES))
                for g in range(chunk)
            ])
            unroll = 4

            def tops(at, row_top):
                for sub in range(unroll):
                    span = pl.ds(pl.multiple_of((at * unroll + sub) * 8, 8), 8)
                    d = cost[pl.ds(base, chunk), span, :]
                    row_top = jnp.maximum(row_top, d + term[span, :][None])
                    peak = jnp.max(d + back, axis=0)
                    old = col_top[span, :]
                    new = jnp.maximum(old, peak)
                    col_top[span, :] = new
                    col_sum[span, :] = col_sum[span, :] * jnp.exp2(old - new)
                return row_top

            row_top = lax.fori_loop(
                0, width // (8 * unroll), tops,
                jnp.full((chunk, 8, LANES), 2 * lowest, jnp.float32),
            )
            row_top = jnp.max(row_top, axis=1, keepdims=True)
            tall = jnp.broadcast_to(row_top, (chunk, 8, LANES))

            def sums(at, state):
                for sub in range(unroll):
                    span = pl.ds(pl.multiple_of((at * unroll + sub) * 8, 8), 8)
                    d = cost[pl.ds(base, chunk), span, :]
                    e = jnp.exp2(d + term[span, :][None] - tall)
                    new = [state[0] + e]
                    if closing:
                        for axis in range(3):
                            new.append(state[1 + axis] + e * place[axis, span, :][None])
                    state = tuple(new)
                    col_sum[span, :] += jnp.sum(
                        jnp.exp2(d + back - col_top[span, :][None]), axis=0
                    )
                return state

            nothing = jnp.zeros((chunk, 8, LANES), jnp.float32)
            state = lax.fori_loop(
                0, width // (8 * unroll), sums, (nothing,) * (4 if closing else 1)
            )
            found = [row_top] + [jnp.sum(value, axis=1, keepdims=True) for value in state]
            for entry, value in enumerate(found):
                for g in range(chunk):
                    send[peer, pl.ds(entry * owned + piece * chunk + g, 1), :] = value[g]

        copies = []
        for step in range(1, cols + 1):
            peer = lax.rem(col_at + step, cols)

            def one(piece, carried, peer=peer):
                visit(peer, piece)
                return carried

            lax.fori_loop(0, pieces, one, 0)
            if turn == 0:
                send[peer, 2 * owned:2 * owned + 8, :] = jnp.broadcast_to(tgt_local, (8, LANES))
            if step < cols:
                copy = pltpu.make_async_remote_copy(
                    src_ref=send.at[peer],
                    dst_ref=take.at[step - 1],
                    send_sem=part_out.at[turn, step - 1],
                    recv_sem=part_in.at[turn, step - 1],
                    device_id=(row_at, peer),
                    device_id_type=MESH,
                )
                copy.start()
                copies.append(copy)

        flat_top = col_top[...].T
        flat_sum = col_sum[...].T
        top = jnp.max(flat_top, axis=0, keepdims=True)
        total = jnp.sum(flat_sum * jnp.exp2(flat_top - top), axis=0, keepdims=True)
        for span in range(spans):
            lanes = slice(span * LANES, (span + 1) * LANES)
            col_send[turn, span:span + 1, :] = top[:, lanes]
            col_send[turn, spans + span:spans + span + 1, :] = total[:, lanes]
        rest = 8 - 2 * spans
        col_send[turn, 2 * spans:8, :] = jnp.broadcast_to(src_local, (rest, LANES))
        crossing = []
        for step in range(1, rows):
            copy = pltpu.make_async_remote_copy(
                src_ref=col_send.at[turn],
                dst_ref=col_take.at[turn, step - 1],
                send_sem=cross_out.at[turn, step - 1],
                recv_sem=cross_in.at[turn, step - 1],
                device_id=(lax.rem(row_at + step, rows), col_at),
                device_id_type=MESH,
            )
            copy.start()
            crossing.append(copy)

        for copy in copies:
            copy.wait_recv()
        count = 5 if closing else 2
        top = send[col_at, 0:owned, :]
        for step in range(cols - 1):
            top = jnp.maximum(top, take[step, 0:owned, :])
        merged = [jnp.zeros((owned, LANES), jnp.float32) for _ in range(count - 1)]
        for step in range(cols):
            def read(low, high, step=step):
                if step == cols - 1:
                    return send[col_at, low:high, :]
                return take[step, low:high, :]

            weight = jnp.exp2(read(0, owned) - top)
            merged = [
                value + weight * read((1 + at) * owned, (2 + at) * owned)
                for at, value in enumerate(merged)
            ]
        if turn == 0:
            mass = tgt_local
            for step in range(cols - 1):
                mass = mass + take[step, 2 * owned:2 * owned + 1, :]
            tgt_log_total = jnp.log2(mass)
        fresh = tgt_log_total - top - jnp.log2(merged[0])
        spread = []
        if closing:
            moved[col_at, 0:owned, :] = fresh * (epsilon / log2e)
            for axis in range(3):
                moved[col_at, (1 + axis) * owned:(2 + axis) * owned, :] = (
                    points[axis, col_at] - merged[1 + axis] / merged[0]
                )
            place_of = moved.at[col_at]
        else:
            if turn > 0:
                fresh = 0.5 * (own[...] + fresh)
            own[...] = fresh
            field[turn + 1, col_at] = masses[col_at] + fresh
            place_of = field.at[turn + 1, col_at]
        for step in range(1, cols):
            copy = pltpu.make_async_remote_copy(
                src_ref=place_of,
                dst_ref=place_of,
                send_sem=whole_out.at[turn, step - 1],
                recv_sem=whole_in.at[turn, step - 1],
                device_id=(row_at, lax.rem(col_at + step, cols)),
                device_id_type=MESH,
            )
            copy.start()
            spread.append(copy)

        for copy in crossing:
            copy.wait_recv()
        top = col_send[turn, 0:spans, :]
        for step in range(rows - 1):
            top = jnp.maximum(top, col_take[turn, step, 0:spans, :])
        total = col_send[turn, spans:2 * spans, :] * jnp.exp2(col_send[turn, 0:spans, :] - top)
        for step in range(rows - 1):
            total = total + col_take[turn, step, spans:2 * spans, :] * jnp.exp2(
                col_take[turn, step, 0:spans, :] - top
            )
        if turn == 0:
            mass = col_send[turn, 2 * spans:2 * spans + 1, :]
            for step in range(rows - 1):
                mass = mass + col_take[turn, step, 2 * spans:2 * spans + 1, :]
            src_log_total = jnp.log2(mass)
        fresh = src_log_total - top - jnp.log2(total)
        if closing:
            tgt_out[...] = fresh * (epsilon / log2e)
        else:
            tgt_field = fresh if turn == 0 else 0.5 * (tgt_field + fresh)
            line = jnp.concatenate(
                [tgt_field[span:span + 1, :] for span in range(spans)], axis=1
            )
            term[...] = columns_of(tgt_log + line)

        for copy in spread:
            copy.wait_recv()
        for copy in copies + crossing + spread:
            copy.wait_send()

    for peer in range(cols):
        span = slice(peer * owned, (peer + 1) * owned)
        src_out[span, :] = moved[peer, 0:owned, :]
        for axis in range(3):
            move_out[axis, span, :] = moved[peer, (1 + axis) * owned:(2 + axis) * owned, :]


def local(rows, cols, src_pos, tgt_pos, src_weight, tgt_weight, src_order, tgt_order, tile_mask):
    count = src_pos.shape[1]
    width = tgt_pos.shape[1]
    groups = count // LANES
    owned = groups // cols
    passes = SWEEPS + 2
    f32 = jnp.float32
    vmem = pl.BlockSpec(memory_space=pltpu.VMEM)
    dma = pltpu.SemaphoreType.DMA
    depths = (2 * owned + 8,) + (2 * owned,) * SWEEPS + (5 * owned,)
    src_out, tgt_out, move_out = pl.pallas_call(
        functools.partial(kernel, rows, cols),
        out_shape=(
            jax.ShapeDtypeStruct((groups, LANES), f32),
            jax.ShapeDtypeStruct((width // LANES, LANES), f32),
            jax.ShapeDtypeStruct((3, groups, LANES), f32),
        ),
        in_specs=[vmem] * 7,
        out_specs=(vmem,) * 3,
        scratch_shapes=[
            pltpu.VMEM((4 * LANES, 2 * groups), jnp.bfloat16),
            pltpu.VMEM((FEATURES, 2 * TILE), f32),
            pltpu.VMEM((16, width), f32),
            pltpu.VMEM((LANES, width), f32),
            pltpu.VMEM((3, cols, owned, LANES), f32),
            pltpu.VMEM((cols, owned, LANES), f32),
            pltpu.VMEM((groups, width, LANES), f32),
            pltpu.VMEM((width, LANES), f32),
            pltpu.VMEM((3, width, LANES), f32),
            pltpu.VMEM((width, LANES), f32),
            pltpu.VMEM((width, LANES), f32),
            pltpu.VMEM((passes, cols, owned, LANES), f32),
            pltpu.VMEM((owned, LANES), f32),
            pltpu.VMEM((cols, 4 * owned, LANES), f32),
            *[pltpu.VMEM((cols, depth, LANES), f32) for depth in depths],
            *[pltpu.VMEM((cols - 1, depth, LANES), f32) for depth in depths],
            pltpu.VMEM((passes, 8, LANES), f32),
            pltpu.VMEM((passes, rows - 1, 8, LANES), f32),
            dma((passes, cols - 1)),
            dma((passes, cols - 1)),
            dma((passes, cols - 1)),
            dma((passes, cols - 1)),
            dma((passes, rows - 1)),
            dma((passes, rows - 1)),
        ],
        compiler_params=pltpu.CompilerParams(
            collective_id=0, has_side_effects=True, vmem_limit_bytes=48 * 2**20
        ),
    )(
        src_pos.reshape(3, groups, LANES),
        src_weight.reshape(groups, LANES),
        src_order.reshape(groups, LANES),
        tgt_pos,
        tgt_weight.reshape(1, width),
        tgt_order.reshape(1, width),
        tile_mask,
    )
    return src_out.reshape(count), tgt_out.reshape(width), move_out.reshape(3, count)


def solution(mesh):
    in_specs = (
        P(None, "row"),
        P(None, "col"),
        P("row"),
        P("col"),
        P("row"),
        P("col"),
        P("row", "col"),
    )
    out_specs = (P("row"), P("col"), P(None, "row"))
    body = functools.partial(local, mesh.shape["row"], mesh.shape["col"])
    return jax.shard_map(body, mesh=mesh, in_specs=in_specs, out_specs=out_specs, check_vma=False)
```

```python
import functools
import math

import jax
import jax.numpy as jnp
from jax import lax
from jax.experimental import pallas as pl
from jax.experimental.pallas import tpu as pltpu
from jax.sharding import PartitionSpec as P

TILE = 256
SWEEPS = 2
LANES = 128
FEATURES = 32
UNROLL = 32

epsilon = 0.4
lowest = -1e30
middle = 5.0
log2e = math.log2(math.e)
scale = 0.5 * log2e / epsilon
MESH = pl.DeviceIdType.MESH


def rounded(x):
    return x.astype(jnp.bfloat16).astype(jnp.float32)


def three(x):
    high = rounded(x)
    mid = rounded(x - high)
    return high, mid, rounded(x - high - mid)


def columns_of(row):
    return jnp.broadcast_to(row, (LANES, row.shape[1])).T


def kernel(
    rows, cols,
    src_pos, src_weight, src_order, tgt_pos, tgt_weight, tgt_order, mask,
    src_out, tgt_out, move_out,
    table, feature, tgt_parts, tgt_feature, points, masses, cost, term, place,
    col_top, col_sum, field, own, moved,
    send_0, send_1, send_2, send_3, take_0, take_1, take_2, take_3, col_send, col_take,
    part_out, part_in, whole_out, whole_in, cross_out, cross_in,
):
    row_at = lax.axis_index("row")
    col_at = lax.axis_index("col")
    sends = (send_0, send_1, send_2, send_3)
    takes = (take_0, take_1, take_2, take_3)
    groups = src_order.shape[0]
    width = tgt_pos.shape[1]
    spans = width // LANES
    owned = field.shape[2]
    chunk = min(8, owned)
    pieces = owned // chunk
    passes = SWEEPS + 2

    barrier = pltpu.get_barrier_semaphore()
    for step in range(1, cols):
        pl.semaphore_signal(
            barrier, inc=1, device_id=(row_at, lax.rem(col_at + step, cols)), device_id_type=MESH
        )
    for step in range(1, rows):
        pl.semaphore_signal(
            barrier, inc=1, device_id=(lax.rem(row_at + step, rows), col_at), device_id_type=MESH
        )

    for entry in range(4):
        value = tgt_weight[...] if entry == 3 else tgt_pos[entry:entry + 1, :] - middle
        for at, part in enumerate(three(value)):
            tgt_parts[4 * at + entry:4 * at + entry + 1, :] = part
    tgt_parts[12:16, :] = jnp.zeros((4, width), jnp.float32)
    chosen = lax.broadcasted_iota(jnp.int32, (width, width), 0) == tgt_order[...] - col_at * width
    picked = jnp.dot(
        tgt_parts[...].astype(jnp.bfloat16),
        chosen.astype(jnp.float32).astype(jnp.bfloat16),
        preferred_element_type=jnp.float32,
    )
    picked = picked[0:4] + picked[4:8] + picked[8:12]
    tgt_feature[...] = jnp.zeros(tgt_feature.shape, jnp.float32)
    norm = jnp.zeros((1, width), jnp.float32)
    for axis in range(3):
        y = picked[axis:axis + 1]
        norm = norm - scale * y * y
        high, mid, low = three(2.0 * scale * y)
        for at, part in enumerate((high, mid, high, low, high, mid)):
            tgt_feature[6 * axis + at:6 * axis + at + 1, :] = part
        place[axis] = columns_of(y)
    for at, part in enumerate(three(norm)):
        tgt_feature[18 + at:19 + at, :] = part
    tgt_feature[21:25, :] = jnp.ones((4, width), jnp.float32)
    tgt_log = jnp.log2(picked[3:4])
    term[...] = columns_of(tgt_log)
    tgt_side = tgt_feature[...].T[:, :FEATURES].astype(jnp.bfloat16)
    tgt_local = jnp.sum(tgt_weight[...], axis=1, keepdims=True)
    src_local = jnp.sum(jnp.sum(src_weight[...], axis=1, keepdims=True), axis=0, keepdims=True)

    for entry in range(4):
        value = src_weight[...] if entry == 3 else src_pos[entry] - middle
        value = value.T
        high = rounded(value)
        span = slice(entry * LANES, (entry + 1) * LANES)
        table[span, 0:groups] = high.astype(jnp.bfloat16)
        table[span, groups:2 * groups] = (value - high).astype(jnp.bfloat16)
    feature[...] = jnp.zeros(feature.shape, jnp.float32)
    batch = feature.shape[1] // LANES

    def fetch(at, carried):
        index = jnp.concatenate(
            [src_order[pl.ds(at * batch + g, 1), :] for g in range(batch)], axis=1
        ) - row_at * (groups * LANES)
        lanes = batch * LANES
        high_at = lax.shift_right_logical(index, 7)
        low_at = lax.bitwise_and(index, LANES - 1)
        hot = lax.broadcasted_iota(jnp.int32, (groups, lanes), 0) == high_at
        hot = hot.astype(jnp.float32).astype(jnp.bfloat16)
        found = jnp.dot(
            table[...], jnp.concatenate([hot, hot], axis=0), preferred_element_type=jnp.float32
        )
        near = lax.broadcasted_iota(jnp.int32, (LANES, lanes), 0) == low_at
        values = [
            jnp.sum(
                jnp.where(near, found[entry * LANES:(entry + 1) * LANES], 0.0),
                axis=0, keepdims=True,
            )
            for entry in range(4)
        ]
        norm = jnp.zeros((1, lanes), jnp.float32)
        for axis in range(3):
            x = values[axis]
            norm = norm - scale * x * x
            high, mid, low = three(x)
            for row, part in enumerate((high, high, mid, high, low, mid)):
                feature[6 * axis + row:6 * axis + row + 1, :] = part
        feature[18:21, :] = jnp.ones((3, lanes), jnp.float32)
        for row, part in enumerate(three(norm)):
            feature[21 + row:22 + row, :] = part
        for tile in range(lanes // TILE):
            kept = mask[pl.ds(at * (lanes // TILE) + tile, 1), :]
            feature[24:25, tile * TILE:(tile + 1) * TILE] = jnp.broadcast_to(
                jnp.where(kept > 0, 0.0, lowest), (1, TILE)
            )
        near_cost = jnp.dot(
            tgt_side, feature[...].astype(jnp.bfloat16), preferred_element_type=jnp.float32
        )
        mass = jnp.log2(values[3])
        for g in range(batch):
            group = at * batch + g
            span = slice(g * LANES, (g + 1) * LANES)
            cost[group] = near_cost[:, span]
            for axis in range(3):
                points[axis, group // owned, pl.ds(lax.rem(group, owned), 1), :] = (
                    values[axis][:, span]
                )
            masses[group // owned, pl.ds(lax.rem(group, owned), 1), :] = mass[:, span]
        return carried

    lax.fori_loop(0, groups // batch, fetch, 0)
    field[0] = masses[...]

    pl.semaphore_wait(barrier, rows + cols - 2)

    src_log_total = None
    tgt_log_total = None
    tgt_field = None
    for turn in range(passes):
        closing = turn == passes - 1
        send = sends[turn]
        take = takes[turn]
        col_top[...] = jnp.full(col_top.shape, lowest, jnp.float32)
        col_sum[...] = jnp.zeros(col_sum.shape, jnp.float32)

        def visit(peer, piece, turn=turn, closing=closing, send=send):
            base = peer * owned + piece * chunk
            back = jnp.stack([
                jnp.broadcast_to(field[turn, peer, pl.ds(piece * chunk + g, 1), :], (8, LANES))
                for g in range(chunk)
            ])
            unroll = min(UNROLL, width // 8)

            def tops(at, row_top):
                for sub in range(unroll):
                    span = pl.ds(pl.multiple_of((at * unroll + sub) * 8, 8), 8)
                    d = cost[pl.ds(base, chunk), span, :]
                    row_top = jnp.maximum(row_top, d + term[span, :][None])
                    peak = jnp.max(d + back, axis=0)
                    old = col_top[span, :]
                    new = jnp.maximum(old, peak)
                    col_top[span, :] = new
                    col_sum[span, :] = col_sum[span, :] * jnp.exp2(old - new)
                return row_top

            row_top = lax.fori_loop(
                0, width // (8 * unroll), tops,
                jnp.full((chunk, 8, LANES), 2 * lowest, jnp.float32),
            )
            row_top = jnp.max(row_top, axis=1, keepdims=True)
            tall = jnp.broadcast_to(row_top, (chunk, 8, LANES))

            def sums(at, state):
                for sub in range(unroll):
                    span = pl.ds(pl.multiple_of((at * unroll + sub) * 8, 8), 8)
                    d = cost[pl.ds(base, chunk), span, :]
                    e = jnp.exp2(d + term[span, :][None] - tall)
                    new = [state[0] + e]
                    if closing:
                        for axis in range(3):
                            new.append(state[1 + axis] + e * place[axis, span, :][None])
                    state = tuple(new)
                    col_sum[span, :] += jnp.sum(
                        jnp.exp2(d + back - col_top[span, :][None]), axis=0
                    )
                return state

            nothing = jnp.zeros((chunk, 8, LANES), jnp.float32)
            state = lax.fori_loop(
                0, width // (8 * unroll), sums, (nothing,) * (4 if closing else 1)
            )
            found = [row_top] + [jnp.sum(value, axis=1, keepdims=True) for value in state]
            for entry, value in enumerate(found):
                for g in range(chunk):
                    send[peer, pl.ds(entry * owned + piece * chunk + g, 1), :] = value[g]

        def sending(step, turn=turn, send=send, take=take):
            peer = lax.rem(col_at + step, cols)
            return pltpu.make_async_remote_copy(
                src_ref=send.at[peer],
                dst_ref=take.at[step - 1],
                send_sem=part_out.at[turn, step - 1],
                recv_sem=part_in.at[turn, step - 1],
                device_id=(row_at, peer),
                device_id_type=MESH,
            )

        def share(step, carried, turn=turn, send=send, sending=sending, visit=visit):
            peer = lax.rem(col_at + step, cols)

            def one(piece, inner):
                visit(peer, piece)
                return inner

            lax.fori_loop(0, pieces, one, 0)
            if turn == 0:
                send[peer, 2 * owned:2 * owned + 8, :] = jnp.broadcast_to(tgt_local, (8, LANES))

            @pl.when(step < cols)
            def _():
                sending(step).start()

            return carried

        lax.fori_loop(1, cols + 1, share, 0)
        copies = [sending(step) for step in range(1, cols)]

        flat_top = col_top[...].T
        flat_sum = col_sum[...].T
        top = jnp.max(flat_top, axis=0, keepdims=True)
        total = jnp.sum(flat_sum * jnp.exp2(flat_top - top), axis=0, keepdims=True)
        for span in range(spans):
            lanes = slice(span * LANES, (span + 1) * LANES)
            col_send[turn, span:span + 1, :] = top[:, lanes]
            col_send[turn, spans + span:spans + span + 1, :] = total[:, lanes]
        rest = 8 - 2 * spans
        col_send[turn, 2 * spans:8, :] = jnp.broadcast_to(src_local, (rest, LANES))
        crossing = []
        for step in range(1, rows):
            copy = pltpu.make_async_remote_copy(
                src_ref=col_send.at[turn],
                dst_ref=col_take.at[turn, step - 1],
                send_sem=cross_out.at[turn, step - 1],
                recv_sem=cross_in.at[turn, step - 1],
                device_id=(lax.rem(row_at + step, rows), col_at),
                device_id_type=MESH,
            )
            copy.start()
            crossing.append(copy)

        for copy in copies:
            copy.wait_recv()
        count = 5 if closing else 2
        top = send[col_at, 0:owned, :]
        for step in range(cols - 1):
            top = jnp.maximum(top, take[step, 0:owned, :])
        merged = [jnp.zeros((owned, LANES), jnp.float32) for _ in range(count - 1)]
        for step in range(cols):
            def read(low, high, step=step):
                if step == cols - 1:
                    return send[col_at, low:high, :]
                return take[step, low:high, :]

            weight = jnp.exp2(read(0, owned) - top)
            merged = [
                value + weight * read((1 + at) * owned, (2 + at) * owned)
                for at, value in enumerate(merged)
            ]
        if turn == 0:
            mass = tgt_local
            for step in range(cols - 1):
                mass = mass + take[step, 2 * owned:2 * owned + 1, :]
            tgt_log_total = jnp.log2(mass)
        fresh = tgt_log_total - top - jnp.log2(merged[0])
        spread = []
        if closing:
            moved[col_at, 0:owned, :] = fresh * (epsilon / log2e)
            for axis in range(3):
                moved[col_at, (1 + axis) * owned:(2 + axis) * owned, :] = (
                    points[axis, col_at] - merged[1 + axis] / merged[0]
                )
            place_of = moved.at[col_at]
        else:
            if turn > 0:
                fresh = 0.5 * (own[...] + fresh)
            own[...] = fresh
            field[turn + 1, col_at] = masses[col_at] + fresh
            place_of = field.at[turn + 1, col_at]
        for step in range(1, cols):
            copy = pltpu.make_async_remote_copy(
                src_ref=place_of,
                dst_ref=place_of,
                send_sem=whole_out.at[turn, step - 1],
                recv_sem=whole_in.at[turn, step - 1],
                device_id=(row_at, lax.rem(col_at + step, cols)),
                device_id_type=MESH,
            )
            copy.start()
            spread.append(copy)

        for copy in crossing:
            copy.wait_recv()
        top = col_send[turn, 0:spans, :]
        for step in range(rows - 1):
            top = jnp.maximum(top, col_take[turn, step, 0:spans, :])
        total = col_send[turn, spans:2 * spans, :] * jnp.exp2(col_send[turn, 0:spans, :] - top)
        for step in range(rows - 1):
            total = total + col_take[turn, step, spans:2 * spans, :] * jnp.exp2(
                col_take[turn, step, 0:spans, :] - top
            )
        if turn == 0:
            mass = col_send[turn, 2 * spans:2 * spans + 1, :]
            for step in range(rows - 1):
                mass = mass + col_take[turn, step, 2 * spans:2 * spans + 1, :]
            src_log_total = jnp.log2(mass)
        fresh = src_log_total - top - jnp.log2(total)
        if closing:
            tgt_out[...] = fresh * (epsilon / log2e)
        else:
            tgt_field = fresh if turn == 0 else 0.5 * (tgt_field + fresh)
            line = jnp.concatenate(
                [tgt_field[span:span + 1, :] for span in range(spans)], axis=1
            )
            term[...] = columns_of(tgt_log + line)

        for copy in spread:
            copy.wait_recv()
        for copy in copies + crossing + spread:
            copy.wait_send()

    for peer in range(cols):
        span = slice(peer * owned, (peer + 1) * owned)
        src_out[span, :] = moved[peer, 0:owned, :]
        for axis in range(3):
            move_out[axis, span, :] = moved[peer, (1 + axis) * owned:(2 + axis) * owned, :]


def local(rows, cols, src_pos, tgt_pos, src_weight, tgt_weight, src_order, tgt_order, tile_mask):
    count = src_pos.shape[1]
    width = tgt_pos.shape[1]
    groups = count // LANES
    owned = groups // cols
    passes = SWEEPS + 2
    f32 = jnp.float32
    vmem = pl.BlockSpec(memory_space=pltpu.VMEM)
    dma = pltpu.SemaphoreType.DMA
    depths = (2 * owned + 8,) + (2 * owned,) * SWEEPS + (5 * owned,)
    src_out, tgt_out, move_out = pl.pallas_call(
        functools.partial(kernel, rows, cols),
        out_shape=(
            jax.ShapeDtypeStruct((groups, LANES), f32),
            jax.ShapeDtypeStruct((width // LANES, LANES), f32),
            jax.ShapeDtypeStruct((3, groups, LANES), f32),
        ),
        in_specs=[vmem] * 7,
        out_specs=(vmem,) * 3,
        scratch_shapes=[
            pltpu.VMEM((4 * LANES, 2 * groups), jnp.bfloat16),
            pltpu.VMEM((FEATURES, 8 * TILE), f32),
            pltpu.VMEM((16, width), f32),
            pltpu.VMEM((LANES, width), f32),
            pltpu.VMEM((3, cols, owned, LANES), f32),
            pltpu.VMEM((cols, owned, LANES), f32),
            pltpu.VMEM((groups, width, LANES), f32),
            pltpu.VMEM((width, LANES), f32),
            pltpu.VMEM((3, width, LANES), f32),
            pltpu.VMEM((width, LANES), f32),
            pltpu.VMEM((width, LANES), f32),
            pltpu.VMEM((passes, cols, owned, LANES), f32),
            pltpu.VMEM((owned, LANES), f32),
            pltpu.VMEM((cols, 4 * owned, LANES), f32),
            *[pltpu.VMEM((cols, depth, LANES), f32) for depth in depths],
            *[pltpu.VMEM((cols - 1, depth, LANES), f32) for depth in depths],
            pltpu.VMEM((passes, 8, LANES), f32),
            pltpu.VMEM((passes, rows - 1, 8, LANES), f32),
            dma((passes, cols - 1)),
            dma((passes, cols - 1)),
            dma((passes, cols - 1)),
            dma((passes, cols - 1)),
            dma((passes, rows - 1)),
            dma((passes, rows - 1)),
        ],
        compiler_params=pltpu.CompilerParams(
            collective_id=0, has_side_effects=True, vmem_limit_bytes=48 * 2**20
        ),
    )(
        src_pos.reshape(3, groups, LANES),
        src_weight.reshape(groups, LANES),
        src_order.reshape(groups, LANES),
        tgt_pos,
        tgt_weight.reshape(1, width),
        tgt_order.reshape(1, width),
        tile_mask,
    )
    return src_out.reshape(count), tgt_out.reshape(width), move_out.reshape(3, count)


def solution(mesh):
    in_specs = (
        P(None, "row"),
        P(None, "col"),
        P("row"),
        P("col"),
        P("row"),
        P("col"),
        P("row", "col"),
    )
    out_specs = (P("row"), P("col"), P(None, "row"))
    body = functools.partial(local, mesh.shape["row"], mesh.shape["col"])
    return jax.shard_map(body, mesh=mesh, in_specs=in_specs, out_specs=out_specs, check_vma=False)
```

```python
import functools
import math

import jax
import jax.numpy as jnp
from jax import lax
from jax.experimental import pallas as pl
from jax.experimental.pallas import tpu as pltpu
from jax.sharding import PartitionSpec as P

TILE = 256
SWEEPS = 2
LANES = 128
FEATURES = 32
UNROLL = 32

epsilon = 0.4
lowest = -1e30
middle = 5.0
log2e = math.log2(math.e)
scale = 0.5 * log2e / epsilon
MESH = pl.DeviceIdType.MESH


def rounded(x):
    return x.astype(jnp.bfloat16).astype(jnp.float32)


def three(x):
    high = rounded(x)
    mid = rounded(x - high)
    return high, mid, rounded(x - high - mid)


def columns_of(row):
    return jnp.broadcast_to(row, (LANES, row.shape[1])).T


def kernel(
    rows, cols,
    src_pos, src_weight, src_order, tgt_pos, tgt_weight, tgt_order, mask,
    src_out, tgt_out, move_out,
    table, feature, tgt_parts, tgt_feature, points, masses, cost, term, place,
    col_top, col_sum, field, own, moved,
    send_0, send_1, send_2, send_3, take_0, take_1, take_2, take_3, col_send, col_take,
    part_out, part_in, whole_out, whole_in, cross_out, cross_in,
):
    row_at = lax.axis_index("row")
    col_at = lax.axis_index("col")
    sends = (send_0, send_1, send_2, send_3)
    takes = (take_0, take_1, take_2, take_3)
    groups = src_order.shape[0]
    width = tgt_pos.shape[1]
    spans = width // LANES
    owned = field.shape[2]
    chunk = min(8, owned)
    pieces = owned // chunk
    passes = SWEEPS + 2

    barrier = pltpu.get_barrier_semaphore()
    for step in range(1, cols):
        pl.semaphore_signal(
            barrier, inc=1, device_id=(row_at, lax.rem(col_at + step, cols)), device_id_type=MESH
        )
    for step in range(1, rows):
        pl.semaphore_signal(
            barrier, inc=1, device_id=(lax.rem(row_at + step, rows), col_at), device_id_type=MESH
        )

    for entry in range(4):
        value = tgt_weight[...] if entry == 3 else tgt_pos[entry:entry + 1, :] - middle
        for at, part in enumerate(three(value)):
            tgt_parts[4 * at + entry:4 * at + entry + 1, :] = part
    tgt_parts[12:16, :] = jnp.zeros((4, width), jnp.float32)
    chosen = lax.broadcasted_iota(jnp.int32, (width, width), 0) == tgt_order[...] - col_at * width
    picked = jnp.dot(
        tgt_parts[...].astype(jnp.bfloat16),
        chosen.astype(jnp.float32).astype(jnp.bfloat16),
        preferred_element_type=jnp.float32,
    )
    picked = picked[0:4] + picked[4:8] + picked[8:12]
    tgt_feature[...] = jnp.zeros(tgt_feature.shape, jnp.float32)
    norm = jnp.zeros((1, width), jnp.float32)
    for axis in range(3):
        y = picked[axis:axis + 1]
        norm = norm - scale * y * y
        high, mid, low = three(2.0 * scale * y)
        for at, part in enumerate((high, mid, high, low, high, mid)):
            tgt_feature[6 * axis + at:6 * axis + at + 1, :] = part
        place[axis] = columns_of(y)
    for at, part in enumerate(three(norm)):
        tgt_feature[18 + at:19 + at, :] = part
    tgt_feature[21:25, :] = jnp.ones((4, width), jnp.float32)
    tgt_log = jnp.log2(picked[3:4])
    term[...] = columns_of(tgt_log)
    tgt_side = tgt_feature[...].T[:, :FEATURES].astype(jnp.bfloat16)
    tgt_local = jnp.sum(tgt_weight[...], axis=1, keepdims=True)
    src_local = jnp.sum(jnp.sum(src_weight[...], axis=1, keepdims=True), axis=0, keepdims=True)

    for entry in range(4):
        value = src_weight[...] if entry == 3 else src_pos[entry] - middle
        value = value.T
        high = rounded(value)
        span = slice(entry * LANES, (entry + 1) * LANES)
        table[span, 0:groups] = high.astype(jnp.bfloat16)
        table[span, groups:2 * groups] = (value - high).astype(jnp.bfloat16)
    feature[...] = jnp.zeros(feature.shape, jnp.float32)
    batch = feature.shape[1] // LANES

    def fetch(at, carried):
        index = jnp.concatenate(
            [src_order[pl.ds(at * batch + g, 1), :] for g in range(batch)], axis=1
        ) - row_at * (groups * LANES)
        lanes = batch * LANES
        high_at = lax.shift_right_logical(index, 7)
        low_at = lax.bitwise_and(index, LANES - 1)
        hot = lax.broadcasted_iota(jnp.int32, (groups, lanes), 0) == high_at
        hot = hot.astype(jnp.float32).astype(jnp.bfloat16)
        found = jnp.dot(
            table[...], jnp.concatenate([hot, hot], axis=0), preferred_element_type=jnp.float32
        )
        near = lax.broadcasted_iota(jnp.int32, (LANES, lanes), 0) == low_at
        values = [
            jnp.sum(
                jnp.where(near, found[entry * LANES:(entry + 1) * LANES], 0.0),
                axis=0, keepdims=True,
            )
            for entry in range(4)
        ]
        norm = jnp.zeros((1, lanes), jnp.float32)
        for axis in range(3):
            x = values[axis]
            norm = norm - scale * x * x
            high, mid, low = three(x)
            for row, part in enumerate((high, high, mid, high, low, mid)):
                feature[6 * axis + row:6 * axis + row + 1, :] = part
        feature[18:21, :] = jnp.ones((3, lanes), jnp.float32)
        for row, part in enumerate(three(norm)):
            feature[21 + row:22 + row, :] = part
        for tile in range(lanes // TILE):
            kept = mask[pl.ds(at * (lanes // TILE) + tile, 1), :]
            feature[24:25, tile * TILE:(tile + 1) * TILE] = jnp.broadcast_to(
                jnp.where(kept > 0, 0.0, lowest), (1, TILE)
            )
        near_cost = jnp.dot(
            tgt_side, feature[...].astype(jnp.bfloat16), preferred_element_type=jnp.float32
        )
        mass = jnp.log2(values[3])
        for g in range(batch):
            group = at * batch + g
            span = slice(g * LANES, (g + 1) * LANES)
            cost[group] = near_cost[:, span]
            for axis in range(3):
                points[axis, group // owned, pl.ds(lax.rem(group, owned), 1), :] = (
                    values[axis][:, span]
                )
            masses[group // owned, pl.ds(lax.rem(group, owned), 1), :] = mass[:, span]
        return carried

    lax.fori_loop(0, groups // batch, fetch, 0)
    field[0] = masses[...]

    pl.semaphore_wait(barrier, rows + cols - 2)

    src_log_total = None
    tgt_log_total = None
    tgt_field = None
    for turn in range(passes):
        closing = turn == passes - 1
        send = sends[turn]
        take = takes[turn]
        col_top[...] = jnp.full(col_top.shape, lowest, jnp.float32)
        col_sum[...] = jnp.zeros(col_sum.shape, jnp.float32)

        def visit(peer, piece, turn=turn, closing=closing, send=send):
            base = peer * owned + piece * chunk
            back = jnp.stack([
                jnp.broadcast_to(field[turn, peer, pl.ds(piece * chunk + g, 1), :], (8, LANES))
                for g in range(chunk)
            ])
            unroll = min(UNROLL, width // 8)

            def tops(at, row_top):
                for sub in range(unroll):
                    span = pl.ds(pl.multiple_of((at * unroll + sub) * 8, 8), 8)
                    d = cost[pl.ds(base, chunk), span, :]
                    row_top = jnp.maximum(row_top, d + term[span, :][None])
                    peak = jnp.max(d + back, axis=0)
                    old = col_top[span, :]
                    new = jnp.maximum(old, peak)
                    col_top[span, :] = new
                    col_sum[span, :] = col_sum[span, :] * jnp.exp2(old - new)
                return row_top

            row_top = lax.fori_loop(
                0, width // (8 * unroll), tops,
                jnp.full((chunk, 8, LANES), 2 * lowest, jnp.float32),
            )
            row_top = jnp.max(row_top, axis=1, keepdims=True)
            tall = jnp.broadcast_to(row_top, (chunk, 8, LANES))

            def sums(at, state):
                for sub in range(unroll):
                    span = pl.ds(pl.multiple_of((at * unroll + sub) * 8, 8), 8)
                    d = cost[pl.ds(base, chunk), span, :]
                    e = jnp.exp2(d + term[span, :][None] - tall)
                    new = [state[0] + e]
                    if closing:
                        for axis in range(3):
                            new.append(state[1 + axis] + e * place[axis, span, :][None])
                    state = tuple(new)
                    col_sum[span, :] += jnp.sum(
                        jnp.exp2(d + back - col_top[span, :][None]), axis=0
                    )
                return state

            nothing = jnp.zeros((chunk, 8, LANES), jnp.float32)
            state = lax.fori_loop(
                0, width // (8 * unroll), sums, (nothing,) * (4 if closing else 1)
            )
            found = [row_top] + [jnp.sum(value, axis=1, keepdims=True) for value in state]
            for entry, value in enumerate(found):
                for g in range(chunk):
                    send[peer, pl.ds(entry * owned + piece * chunk + g, 1), :] = value[g]

        def sending(step, turn=turn, send=send, take=take):
            peer = lax.rem(col_at + step, cols)
            return pltpu.make_async_remote_copy(
                src_ref=send.at[peer],
                dst_ref=take.at[step - 1],
                send_sem=part_out.at[turn, step - 1],
                recv_sem=part_in.at[turn, step - 1],
                device_id=(row_at, peer),
                device_id_type=MESH,
            )

        def share(step, carried, turn=turn, send=send, sending=sending, visit=visit):
            peer = lax.rem(col_at + step, cols)

            def one(piece, inner):
                visit(peer, piece)
                return inner

            lax.fori_loop(0, pieces, one, 0)
            if turn == 0:
                send[peer, 2 * owned:2 * owned + 8, :] = jnp.broadcast_to(tgt_local, (8, LANES))

            @pl.when(step < cols)
            def _():
                sending(step).start()

            return carried

        lax.fori_loop(1, cols + 1, share, 0)
        copies = [sending(step) for step in range(1, cols)]

        flat_top = col_top[...].T
        flat_sum = col_sum[...].T
        top = jnp.max(flat_top, axis=0, keepdims=True)
        total = jnp.sum(flat_sum * jnp.exp2(flat_top - top), axis=0, keepdims=True)
        for span in range(spans):
            lanes = slice(span * LANES, (span + 1) * LANES)
            col_send[turn, span:span + 1, :] = top[:, lanes]
            col_send[turn, spans + span:spans + span + 1, :] = total[:, lanes]
        rest = 8 - 2 * spans
        col_send[turn, 2 * spans:8, :] = jnp.broadcast_to(src_local, (rest, LANES))
        crossing = []
        for step in range(1, rows):
            copy = pltpu.make_async_remote_copy(
                src_ref=col_send.at[turn],
                dst_ref=col_take.at[turn, step - 1],
                send_sem=cross_out.at[turn, step - 1],
                recv_sem=cross_in.at[turn, step - 1],
                device_id=(lax.rem(row_at + step, rows), col_at),
                device_id_type=MESH,
            )
            copy.start()
            crossing.append(copy)

        for copy in copies:
            copy.wait_recv()
        count = 5 if closing else 2
        top = send[col_at, 0:owned, :]
        for step in range(cols - 1):
            top = jnp.maximum(top, take[step, 0:owned, :])
        merged = [jnp.zeros((owned, LANES), jnp.float32) for _ in range(count - 1)]
        for step in range(cols):
            def read(low, high, step=step):
                if step == cols - 1:
                    return send[col_at, low:high, :]
                return take[step, low:high, :]

            weight = jnp.exp2(read(0, owned) - top)
            merged = [
                value + weight * read((1 + at) * owned, (2 + at) * owned)
                for at, value in enumerate(merged)
            ]
        if turn == 0:
            mass = tgt_local
            for step in range(cols - 1):
                mass = mass + take[step, 2 * owned:2 * owned + 1, :]
            tgt_log_total = jnp.log2(mass)
        fresh = tgt_log_total - top - jnp.log2(merged[0])
        spread = []
        if closing:
            moved[col_at, 0:owned, :] = fresh * (epsilon / log2e)
            for axis in range(3):
                moved[col_at, (1 + axis) * owned:(2 + axis) * owned, :] = (
                    points[axis, col_at] - merged[1 + axis] / merged[0]
                )
            place_of = moved.at[col_at]
        else:
            if turn > 0:
                fresh = 0.5 * (own[...] + fresh)
            own[...] = fresh
            field[turn + 1, col_at] = masses[col_at] + fresh
            place_of = field.at[turn + 1, col_at]
        for step in range(1, cols):
            copy = pltpu.make_async_remote_copy(
                src_ref=place_of,
                dst_ref=place_of,
                send_sem=whole_out.at[turn, step - 1],
                recv_sem=whole_in.at[turn, step - 1],
                device_id=(row_at, lax.rem(col_at + step, cols)),
                device_id_type=MESH,
            )
            copy.start()
            spread.append(copy)

        for copy in crossing:
            copy.wait_recv()
        top = col_send[turn, 0:spans, :]
        for step in range(rows - 1):
            top = jnp.maximum(top, col_take[turn, step, 0:spans, :])
        total = col_send[turn, spans:2 * spans, :] * jnp.exp2(col_send[turn, 0:spans, :] - top)
        for step in range(rows - 1):
            total = total + col_take[turn, step, spans:2 * spans, :] * jnp.exp2(
                col_take[turn, step, 0:spans, :] - top
            )
        if turn == 0:
            mass = col_send[turn, 2 * spans:2 * spans + 1, :]
            for step in range(rows - 1):
                mass = mass + col_take[turn, step, 2 * spans:2 * spans + 1, :]
            src_log_total = jnp.log2(mass)
        fresh = src_log_total - top - jnp.log2(total)
        if closing:
            tgt_out[...] = fresh * (epsilon / log2e)
        else:
            tgt_field = fresh if turn == 0 else 0.5 * (tgt_field + fresh)
            line = jnp.concatenate(
                [tgt_field[span:span + 1, :] for span in range(spans)], axis=1
            )
            term[...] = columns_of(tgt_log + line)

        for copy in spread:
            copy.wait_recv()
        for copy in copies + crossing + spread:
            copy.wait_send()

    for peer in range(cols):
        span = slice(peer * owned, (peer + 1) * owned)
        src_out[span, :] = moved[peer, 0:owned, :]
        for axis in range(3):
            move_out[axis, span, :] = moved[peer, (1 + axis) * owned:(2 + axis) * owned, :]


def local(rows, cols, src_pos, tgt_pos, src_weight, tgt_weight, src_order, tgt_order, tile_mask):
    count = src_pos.shape[1]
    width = tgt_pos.shape[1]
    groups = count // LANES
    owned = groups // cols
    passes = SWEEPS + 2
    f32 = jnp.float32
    vmem = pl.BlockSpec(memory_space=pltpu.VMEM)
    dma = pltpu.SemaphoreType.DMA
    depths = (2 * owned + 8,) + (2 * owned,) * SWEEPS + (5 * owned,)
    src_out, tgt_out, move_out = pl.pallas_call(
        functools.partial(kernel, rows, cols),
        out_shape=(
            jax.ShapeDtypeStruct((groups, LANES), f32),
            jax.ShapeDtypeStruct((width // LANES, LANES), f32),
            jax.ShapeDtypeStruct((3, groups, LANES), f32),
        ),
        in_specs=[vmem] * 7,
        out_specs=(vmem,) * 3,
        scratch_shapes=[
            pltpu.VMEM((4 * LANES, 2 * groups), jnp.bfloat16),
            pltpu.VMEM((FEATURES, 16 * TILE), f32),
            pltpu.VMEM((16, width), f32),
            pltpu.VMEM((LANES, width), f32),
            pltpu.VMEM((3, cols, owned, LANES), f32),
            pltpu.VMEM((cols, owned, LANES), f32),
            pltpu.VMEM((groups, width, LANES), f32),
            pltpu.VMEM((width, LANES), f32),
            pltpu.VMEM((3, width, LANES), f32),
            pltpu.VMEM((width, LANES), f32),
            pltpu.VMEM((width, LANES), f32),
            pltpu.VMEM((passes, cols, owned, LANES), f32),
            pltpu.VMEM((owned, LANES), f32),
            pltpu.VMEM((cols, 4 * owned, LANES), f32),
            *[pltpu.VMEM((cols, depth, LANES), f32) for depth in depths],
            *[pltpu.VMEM((cols - 1, depth, LANES), f32) for depth in depths],
            pltpu.VMEM((passes, 8, LANES), f32),
            pltpu.VMEM((passes, rows - 1, 8, LANES), f32),
            dma((passes, cols - 1)),
            dma((passes, cols - 1)),
            dma((passes, cols - 1)),
            dma((passes, cols - 1)),
            dma((passes, rows - 1)),
            dma((passes, rows - 1)),
        ],
        compiler_params=pltpu.CompilerParams(
            collective_id=0, has_side_effects=True, vmem_limit_bytes=48 * 2**20
        ),
    )(
        src_pos.reshape(3, groups, LANES),
        src_weight.reshape(groups, LANES),
        src_order.reshape(groups, LANES),
        tgt_pos,
        tgt_weight.reshape(1, width),
        tgt_order.reshape(1, width),
        tile_mask,
    )
    return src_out.reshape(count), tgt_out.reshape(width), move_out.reshape(3, count)


def solution(mesh):
    in_specs = (
        P(None, "row"),
        P(None, "col"),
        P("row"),
        P("col"),
        P("row"),
        P("col"),
        P("row", "col"),
    )
    out_specs = (P("row"), P("col"), P(None, "row"))
    body = functools.partial(local, mesh.shape["row"], mesh.shape["col"])
    return jax.shard_map(body, mesh=mesh, in_specs=in_specs, out_specs=out_specs, check_vma=False)
```
